32 devices in a mesh: groups: 2 (over y), wid: 4 (over z), ffn: 4 (over x, core).
Axes of the slice: x: 2, y: 2, z: 4, core: 2. Of those that a mesh axis runs over, the one named last changes fastest.
Arguments:
- tokens: bfloat16 [256, 16384], P(('groups', 'ffn'), 'wid'), parts along dimension 0, may hold values from -6 to 6
- gate_blocks: bfloat16 [4, 4, 815, 128, 128], P('wid', 'ffn'), may hold values from -0.0625 to 0.0625
- gate_slots: int32 [4, 4, 815], P('wid', 'ffn'), may hold values from 0 to 1663, as said below
- gate_count: int32 [4, 4], P('wid', 'ffn'), may hold values from 416 to 815, as said below
- up_blocks: bfloat16 [4, 4, 815, 128, 128], P('wid', 'ffn'), may hold values from -0.0625 to 0.0625
- up_slots: int32 [4, 4, 815], P('wid', 'ffn'), may hold values from 0 to 1663, as said below
- up_count: int32 [4, 4], P('wid', 'ffn'), may hold values from 416 to 815, as said below
- down_blocks: bfloat16 [4, 4, 815, 128, 128], P('ffn', 'wid'), may hold values from -0.0546875 to 0.0546875
- down_slots: int32 [4, 4, 815], P('ffn', 'wid'), may hold values from 0 to 1663, as said below
- down_count: int32 [4, 4], P('ffn', 'wid'), may hold values from 416 to 815, as said below
Outputs:
- mixed: bfloat16 [256, 16384], P(('groups', 'ffn'), 'wid'), parts along dimension 0
The draws below stay inside these ranges and needn't reach their ends.
There are 2 independent parts, one for each index of `groups`. The reference program is written for one: setup_inputs(seed, part) draws one part's arguments, and reference() takes and returns one part's arrays. A program takes and returns all parts, laid end to end along the dimension named above; an argument that names none is the same for every part. Nothing has to cross between parts.
Inputs may be any that keep to these rules, and one draw needn't show every extreme that they name: `gate_slots`: each tile's 815 entries are distinct block positions of that tile; only the first count entries are kept. `gate_count`: some tile keeps 815 blocks in every draw. `up_slots`: each tile's 815 entries are distinct block positions of that tile; only the first count entries are kept. `up_count`: some tile keeps 815 blocks in every draw. `down_slots`: each tile's 815 entries are distinct block positions of that tile; only the first count entries are kept. `down_count`: some tile keeps 815 blocks in every draw.
All inputs are finite; a program needn't handle non-finite values.
Results may differ from the reference program's by a relative error of at most 0.02.
Values may be sent and summed in bfloat16 or wider, within the bound.
A program may use at most 320 MiB of HBM per device.

```python
import jax
import jax.numpy as jnp
from jax import lax

D = 16384
FF = 26624
BLK = 128
TOKENS = 128
DTILE = 4096
FTILE = 6656
TILE_BLOCKS = 1664
MAXB = 815
N_WID = 4
N_FFN = 4


def count_table(key, leading, trailing):
    first, second, third = jax.random.split(key, 3)
    total = leading * trailing
    drawn = jax.random.randint(first, (total,), TILE_BLOCKS // 4, MAXB + 1, dtype=jnp.int32)
    heavy = jax.random.randint(second, (total,), 0, 8, dtype=jnp.int32) == 0
    counts = jnp.where(heavy, MAXB, drawn)
    chosen = jax.random.randint(third, (), 0, total, dtype=jnp.int32)
    counts = jnp.where(jnp.arange(total, dtype=jnp.int32) == chosen, MAXB, counts)
    return counts.reshape(leading, trailing).astype(jnp.int32)


def one_list(subkey):
    return jax.random.permutation(subkey, TILE_BLOCKS)[:MAXB]


def slot_table(key, leading, trailing):
    subkeys = jax.random.split(key, leading * trailing)
    lists = jax.vmap(one_list)(subkeys)
    return lists.reshape(leading, trailing, MAXB).astype(jnp.int32)


def draw_gate_slots(key, part):
    key = jax.random.fold_in(key, 11)
    return slot_table(key, N_WID, N_FFN)


def draw_gate_count(key, part):
    key = jax.random.fold_in(key, 12)
    return count_table(key, N_WID, N_FFN)


def draw_up_slots(key, part):
    key = jax.random.fold_in(key, 21)
    return slot_table(key, N_WID, N_FFN)


def draw_up_count(key, part):
    key = jax.random.fold_in(key, 22)
    return count_table(key, N_WID, N_FFN)


def draw_down_slots(key, part):
    key = jax.random.fold_in(key, 31)
    return slot_table(key, N_FFN, N_WID)


def draw_down_count(key, part):
    key = jax.random.fold_in(key, 32)
    return count_table(key, N_FFN, N_WID)


def levels(rng, shape, cuts, least, largest):
    gain = 1.0
    for dim, parts in cuts:
        heights = jax.random.uniform(jax.random.fold_in(jax.random.fold_in(rng, 6), dim), (parts,), jnp.float32, least / len(cuts), largest / len(cuts))
        gain = gain * jnp.repeat(jnp.exp(heights), shape[dim] // parts).reshape((-1,) + (1,) * (len(shape) - 1 - dim))
    return gain


def gaussian(own_key, shape, width, bound, cuts=(), kind=jnp.bfloat16):
    level = levels(own_key, shape, cuts, -0.22, 0.18) if cuts else 1.0
    array = jax.random.normal(own_key, shape, jnp.float32) * width * level
    return jnp.minimum(jnp.maximum(array, -bound), bound).astype(kind)


def setup_inputs(seed: int = 0, part: int = 0) -> dict:
    key_of = jax.random.split(jax.random.key(seed), 11)
    part_splits = jax.random.split(jax.random.fold_in(key_of[10], part), 11)
    tokens = gaussian(part_splits[0], (TOKENS, D), 1.0, 6.0, ((0, 4), (1, 4)))
    gate_blocks = gaussian(key_of[1], (N_WID, N_FFN, MAXB, BLK, BLK), (D // 2) ** -0.5, 0.0625, ((0, 4), (1, 4)))
    gate_slots = draw_gate_slots(jax.random.fold_in(key_of[10], 71), part)
    gate_count = draw_gate_count(jax.random.fold_in(key_of[10], 71), part)
    up_blocks = gaussian(key_of[4], (N_WID, N_FFN, MAXB, BLK, BLK), (D // 2) ** -0.5, 0.0625, ((0, 4), (1, 4)))
    up_slots = draw_up_slots(jax.random.fold_in(key_of[10], 71), part)
    up_count = draw_up_count(jax.random.fold_in(key_of[10], 71), part)
    down_blocks = gaussian(key_of[7], (N_FFN, N_WID, MAXB, BLK, BLK), (FF // 2) ** -0.5, 0.0546875, ((0, 4), (1, 4)))
    down_slots = draw_down_slots(jax.random.fold_in(key_of[10], 71), part)
    down_count = draw_down_count(jax.random.fold_in(key_of[10], 71), part)
    return {"tokens": tokens, "gate_blocks": gate_blocks, "gate_slots": gate_slots, "gate_count": gate_count, "up_blocks": up_blocks, "up_slots": up_slots, "up_count": up_count, "down_blocks": down_blocks, "down_slots": down_slots, "down_count": down_count}


def rounded(values):
    return lax.optimization_barrier(values.astype(jnp.bfloat16)).astype(jnp.float32)


def tile_product(operand, blocks, slots, kept, out_blocks):
    row_count = operand.shape[0]
    block_size = blocks.shape[-1]
    in_blocks = operand.shape[1] // block_size
    pieces = jnp.take(operand.reshape(row_count, in_blocks, block_size), slots // out_blocks, axis=1)
    products = jnp.einsum("tbk,bkn->tbn", pieces.astype(jnp.float32), blocks.astype(jnp.float32), precision=lax.Precision.HIGHEST)
    is_kept = jnp.arange(slots.shape[0], dtype=jnp.int32) < kept
    placement = (((slots % out_blocks)[:, None] == jnp.arange(out_blocks, dtype=jnp.int32)[None, :]) & is_kept[:, None]).astype(jnp.float32)
    summed = jnp.einsum("tbn,bo->ton", products, placement, precision=lax.Precision.HIGHEST)
    return summed.reshape(row_count, out_blocks * block_size)


def reference(tokens, gate_blocks, gate_slots, gate_count, up_blocks, up_slots, up_count, down_blocks, down_slots, down_count):
    ffn_blocks = FTILE // BLK
    wid_blocks = DTILE // BLK

    def hidden_column(col_tile):
        def add_row(totals, row_tile):
            operand = lax.dynamic_slice_in_dim(tokens, (row_tile * DTILE).astype(jnp.int32), DTILE, 1)
            gate_part = tile_product(operand, gate_blocks[row_tile, col_tile], gate_slots[row_tile, col_tile], gate_count[row_tile, col_tile], ffn_blocks)
            up_part = tile_product(operand, up_blocks[row_tile, col_tile], up_slots[row_tile, col_tile], up_count[row_tile, col_tile], ffn_blocks)
            return (totals[0] + rounded(gate_part), totals[1] + rounded(up_part)), None

        initial = jnp.zeros((TOKENS, FTILE), jnp.float32)
        (gate, up), _ = lax.scan(add_row, (initial, initial), jnp.arange(N_WID, dtype=jnp.int32))
        return (jax.nn.silu(gate) * up).astype(jnp.bfloat16)

    hidden = lax.map(hidden_column, jnp.arange(N_FFN, dtype=jnp.int32))

    def output_column(row_tile):
        def add_part(total, col_tile):
            part = tile_product(hidden[col_tile], down_blocks[col_tile, row_tile], down_slots[col_tile, row_tile], down_count[col_tile, row_tile], wid_blocks)
            return total + rounded(part), None

        total, _ = lax.scan(add_part, jnp.zeros((TOKENS, DTILE), jnp.float32), jnp.arange(N_FFN, dtype=jnp.int32))
        return total.astype(jnp.bfloat16)

    columns = lax.map(output_column, jnp.arange(N_WID, dtype=jnp.int32))
    return jnp.transpose(columns, (1, 0, 2)).reshape(TOKENS, D)
```

```python
import functools

import jax
import jax.numpy as jnp
from jax import lax
from jax.experimental import pallas as pl
from jax.experimental.pallas import tpu as pltpu
from jax.sharding import PartitionSpec as P

FF = 26624
GROUP = 4
BATCH = 4
STEP = GROUP * BATCH
DEPTH = 8


def block_lists(slots, kept, in_blocks, out_blocks):
    count = slots.shape[0]
    index = jnp.arange(count, dtype=jnp.int32)
    is_kept = index < kept
    col = jnp.where(is_kept, slots % out_blocks, out_blocks)
    row = slots // out_blocks
    rank = jnp.sum(
        (col[None, :] == col[:, None]) & (index[None, :] < index[:, None]), axis=1, dtype=jnp.int32
    )
    columns = jnp.arange(out_blocks, dtype=jnp.int32)
    number = jnp.sum(col[None, :] == columns[:, None], axis=1, dtype=jnp.int32)
    groups = (number + GROUP - 1) // GROUP
    ends = jnp.sum(
        jnp.where(columns[None, :] <= columns[:, None], groups[None, :], 0), axis=1, dtype=jnp.int32
    )
    first = jnp.sum(
        jnp.where(columns[None, :] < col[:, None], groups[None, :], 0), axis=1, dtype=jnp.int32
    )
    place = jnp.where(is_kept, first * GROUP + rank, -1)
    most = (count + out_blocks * (GROUP - 1)) // GROUP
    most = -(-most // BATCH) * BATCH
    match = place[None, :] == jnp.arange(most * GROUP, dtype=jnp.int32)[:, None]
    packed = jnp.sum(
        jnp.where(match, (index * in_blocks + row + 1)[None, :], 0), axis=1, dtype=jnp.int32
    )
    order = jnp.where(packed > 0, (packed - 1) // in_blocks, 0)
    rows = jnp.where(packed > 0, (packed - 1) % in_blocks, in_blocks)
    cols = jnp.sum(
        ends[None, :] <= jnp.arange(most, dtype=jnp.int32)[:, None], axis=1, dtype=jnp.int32
    )
    cols = jnp.minimum(cols, out_blocks - 1)
    batches = (ends[-1:] + BATCH - 1) // BATCH
    return order, rows, cols, batches


def tile_kernel(matrices, *refs):
    lists = refs[: 4 * matrices]
    x_ref = refs[4 * matrices]
    blocks = refs[4 * matrices + 1 : 5 * matrices + 1]
    out_ref, pieces, total, held, sems = refs[5 * matrices + 1 :]
    in_blocks = pieces.shape[0] - 1
    out_blocks = total.shape[0]

    def start(m, step):
        order = lists[4 * m]
        slot = lax.rem(step, DEPTH)
        for i in range(STEP):
            pltpu.make_async_copy(
                blocks[m].at[order[step * STEP + i]], held.at[m, slot, i], sems.at[m, slot]
            ).start()

    for m in range(matrices):

        @pl.loop(0, jnp.minimum(lists[4 * m + 3][0], DEPTH))
        def _(step):
            start(m, step)

    for i in range(in_blocks):
        pieces[i] = x_ref[:, i * 128 : (i + 1) * 128]
    pieces[in_blocks] = jnp.zeros(pieces.shape[1:], pieces.dtype)

    for m in range(matrices):
        rows, cols = lists[4 * m + 1], lists[4 * m + 2]
        batches = lists[4 * m + 3][0]

        @pl.loop(0, out_blocks)
        def _(o):
            total[o] = jnp.zeros(total.shape[1:], total.dtype)

        @pl.loop(0, batches)
        def _(step):
            slot = lax.rem(step, DEPTH)
            pltpu.make_async_copy(
                blocks[m].at[pl.ds(0, STEP)], held.at[m, slot], sems.at[m, slot]
            ).wait()
            for u in range(BATCH):
                base = step * STEP + u * GROUP
                piece = jnp.concatenate([pieces[rows[base + i]] for i in range(GROUP)], axis=1)
                weight = held[m, slot, u * GROUP : (u + 1) * GROUP].reshape(GROUP * 128, 128)
                product = jnp.dot(piece, weight, preferred_element_type=jnp.float32)
                o = cols[step * BATCH + u]
                total[o] = total[o] + product

            @pl.when(step + DEPTH < batches)
            def _():
                start(m, step + DEPTH)

        for o in range(out_blocks):
            at = (m * out_blocks + o) * 128
            out_ref[:, at : at + 128] = total[o].astype(out_ref.dtype)


def tile_products(operand, parts, out_blocks):
    tokens, width = operand.shape
    in_blocks = width // 128
    matrices = len(parts)
    lists = []
    for blocks, slots, kept in parts:
        lists += block_lists(slots, kept, in_blocks, out_blocks)
    count = parts[0][0].shape[0]
    smem = pl.BlockSpec(memory_space=pltpu.SMEM)
    vmem = pl.BlockSpec(memory_space=pltpu.VMEM)
    return pl.pallas_call(
        functools.partial(tile_kernel, matrices),
        out_shape=jax.ShapeDtypeStruct((tokens, matrices * out_blocks * 128), jnp.bfloat16),
        in_specs=[smem] * (4 * matrices) + [vmem] + [pl.BlockSpec(memory_space=pl.ANY)] * matrices,
        out_specs=vmem,
        scratch_shapes=[
            pltpu.VMEM((in_blocks + 1, tokens, 128), jnp.bfloat16),
            pltpu.VMEM((out_blocks, tokens, 128), jnp.float32),
            pltpu.VMEM((matrices, DEPTH, STEP, 128, 128), jnp.bfloat16),
            pltpu.SemaphoreType.DMA((matrices, DEPTH)),
        ],
        compiler_params=pltpu.CompilerParams(vmem_limit_bytes=50 * 1024 * 1024),
        cost_estimate=pl.CostEstimate(
            flops=2 * tokens * 128 * 128 * count * matrices,
            bytes_accessed=2 * 128 * 128 * count * matrices,
            transcendentals=0,
        ),
    )(*lists, operand, *[blocks for blocks, _, _ in parts])


def on_device(
    tokens,
    gate_blocks,
    gate_slots,
    gate_count,
    up_blocks,
    up_slots,
    up_count,
    down_blocks,
    down_slots,
    down_count,
):
    ffn_blocks = FF // lax.axis_size("ffn") // 128
    wid_blocks = tokens.shape[1] // 128
    full_tokens = lax.all_gather(tokens, "ffn", axis=0, tiled=True)
    partial = tile_products(
        full_tokens,
        [
            (gate_blocks[0, 0], gate_slots[0, 0], gate_count[0, 0]),
            (up_blocks[0, 0], up_slots[0, 0], up_count[0, 0]),
        ],
        ffn_blocks,
    )
    sums_both = lax.psum_scatter(partial, "wid", scatter_dimension=0, tiled=True).astype(jnp.float32)
    half_width = sums_both.shape[1] // 2
    hidden_share = (jax.nn.silu(sums_both[:, :half_width]) * sums_both[:, half_width:]).astype(
        jnp.bfloat16
    )
    hidden = lax.all_gather(hidden_share, "wid", axis=0, tiled=True)
    mixed = tile_products(
        hidden, [(down_blocks[0, 0], down_slots[0, 0], down_count[0, 0])], wid_blocks
    )
    return lax.psum_scatter(mixed, "ffn", scatter_dimension=0, tiled=True)


def solution(mesh):
    return jax.shard_map(
        on_device,
        mesh=mesh,
        in_specs=(
            P(("groups", "ffn"), "wid"),
            P("wid", "ffn", None, None, None),
            P("wid", "ffn", None),
            P("wid", "ffn"),
            P("wid", "ffn", None, None, None),
            P("wid", "ffn", None),
            P("wid", "ffn"),
            P("ffn", "wid", None, None, None),
            P("ffn", "wid", None),
            P("ffn", "wid"),
        ),
        out_specs=P(("groups", "ffn"), "wid"),
        check_vma=False,
    )
```

```python
import functools

import jax
import jax.numpy as jnp
from jax import lax
from jax.experimental import pallas as pl
from jax.experimental.pallas import tpu as pltpu
from jax.sharding import PartitionSpec as P

FF = 26624
GROUP = 4
BATCH = 4
STEP = GROUP * BATCH
DEPTH = 8


def block_lists(slots, kept, in_blocks, out_blocks):
    count = slots.shape[0]
    index = jnp.arange(count, dtype=jnp.int32)
    is_kept = index < kept
    col = jnp.where(is_kept, slots % out_blocks, out_blocks)
    row = slots // out_blocks
    rank = jnp.sum(
        (col[None, :] == col[:, None]) & (index[None, :] < index[:, None]), axis=1, dtype=jnp.int32
    )
    columns = jnp.arange(out_blocks, dtype=jnp.int32)
    number = jnp.sum(col[None, :] == columns[:, None], axis=1, dtype=jnp.int32)
    groups = (number + GROUP - 1) // GROUP
    ends = jnp.sum(
        jnp.where(columns[None, :] <= columns[:, None], groups[None, :], 0), axis=1, dtype=jnp.int32
    )
    first = jnp.sum(
        jnp.where(columns[None, :] < col[:, None], groups[None, :], 0), axis=1, dtype=jnp.int32
    )
    place = jnp.where(is_kept, first * GROUP + rank, -1)
    most = (count + out_blocks * (GROUP - 1)) // GROUP
    most = -(-most // BATCH) * BATCH
    match = place[None, :] == jnp.arange(most * GROUP, dtype=jnp.int32)[:, None]
    packed = jnp.sum(
        jnp.where(match, (index * in_blocks + row + 1)[None, :], 0), axis=1, dtype=jnp.int32
    )
    order = jnp.where(packed > 0, (packed - 1) // in_blocks, 0)
    rows = jnp.where(packed > 0, (packed - 1) % in_blocks, in_blocks)
    cols = jnp.sum(
        ends[None, :] <= jnp.arange(most, dtype=jnp.int32)[:, None], axis=1, dtype=jnp.int32
    )
    cols = jnp.minimum(cols, out_blocks - 1)
    batches = (ends[-1:] + BATCH - 1) // BATCH
    return order, rows, cols, batches


def tile_kernel(matrices, *refs):
    lists = refs[: 4 * matrices]
    x_ref = refs[4 * matrices]
    blocks = refs[4 * matrices + 1 : 5 * matrices + 1]
    out_ref, pieces, total, held, sems = refs[5 * matrices + 1 :]
    in_blocks = pieces.shape[0] - 1
    out_blocks = total.shape[0]

    def start(m, step):
        order = lists[4 * m]
        slot = lax.rem(step, DEPTH)
        for i in range(STEP):
            pltpu.make_async_copy(
                blocks[m].at[order[step * STEP + i]], held.at[m, slot, i], sems.at[m, slot]
            ).start()

    for m in range(matrices):

        @pl.loop(0, jnp.minimum(lists[4 * m + 3][0], DEPTH))
        def _(step):
            start(m, step)

    for i in range(in_blocks):
        per = x_ref.shape[2] // 128
        pieces[i] = x_ref[i // per, :, i % per * 128 : (i % per + 1) * 128]
    pieces[in_blocks] = jnp.zeros(pieces.shape[1:], pieces.dtype)

    for m in range(matrices):
        rows, cols = lists[4 * m + 1], lists[4 * m + 2]
        batches = lists[4 * m + 3][0]

        @pl.loop(0, out_blocks)
        def _(o):
            total[o] = jnp.zeros(total.shape[1:], total.dtype)

        @pl.loop(0, batches)
        def _(step):
            slot = lax.rem(step, DEPTH)
            pltpu.make_async_copy(
                blocks[m].at[pl.ds(0, STEP)], held.at[m, slot], sems.at[m, slot]
            ).wait()
            for u in range(BATCH):
                base = step * STEP + u * GROUP
                piece = jnp.concatenate([pieces[rows[base + i]] for i in range(GROUP)], axis=1)
                weight = held[m, slot, u * GROUP : (u + 1) * GROUP].reshape(GROUP * 128, 128)
                product = jnp.dot(piece, weight, preferred_element_type=jnp.float32)
                o = cols[step * BATCH + u]
                total[o] = total[o] + product

            @pl.when(step + DEPTH < batches)
            def _():
                start(m, step + DEPTH)

        for o in range(out_blocks):
            per = out_ref.shape[3] // 128
            at = o % per * 128
            out_ref[o // per, m, :, at : at + 128] = total[o].astype(out_ref.dtype)


def tile_products(operand, parts, out_blocks, chunks):
    tokens = operand.shape[1]
    in_blocks = operand.shape[0] * operand.shape[2] // 128
    matrices = len(parts)
    lists = []
    for blocks, slots, kept in parts:
        lists += block_lists(slots, kept, in_blocks, out_blocks)
    count = parts[0][0].shape[0]
    smem = pl.BlockSpec(memory_space=pltpu.SMEM)
    vmem = pl.BlockSpec(memory_space=pltpu.VMEM)
    return pl.pallas_call(
        functools.partial(tile_kernel, matrices),
        out_shape=jax.ShapeDtypeStruct(
            (chunks, matrices, tokens, out_blocks * 128 // chunks), jnp.bfloat16
        ),
        in_specs=[smem] * (4 * matrices) + [vmem] + [pl.BlockSpec(memory_space=pl.ANY)] * matrices,
        out_specs=vmem,
        scratch_shapes=[
            pltpu.VMEM((in_blocks + 1, tokens, 128), jnp.bfloat16),
            pltpu.VMEM((out_blocks, tokens, 128), jnp.float32),
            pltpu.VMEM((matrices, DEPTH, STEP, 128, 128), jnp.bfloat16),
            pltpu.SemaphoreType.DMA((matrices, DEPTH)),
        ],
        compiler_params=pltpu.CompilerParams(vmem_limit_bytes=50 * 1024 * 1024),
        cost_estimate=pl.CostEstimate(
            flops=2 * tokens * 128 * 128 * count * matrices,
            bytes_accessed=2 * 128 * 128 * count * matrices,
            transcendentals=0,
        ),
    )(*lists, operand, *[blocks for blocks, _, _ in parts])


def hidden_kernel(n, part_ref, hid_ref, sums, send_sem, recv_sem, back_sem, home_sem):
    me = lax.axis_index("wid")
    chunks, _, tokens, _ = part_ref.shape
    half = tokens // 2
    lag = min(n, chunks)

    barrier = pltpu.get_barrier_semaphore()
    for exists, other in ((me > 0, me - 1), (me < n - 1, me + 1)):

        @pl.when(exists)
        def _():
            pl.semaphore_signal(
                barrier, inc=1, device_id={"wid": other}, device_id_type=pl.DeviceIdType.MESH
            )

    pl.semaphore_wait(barrier, jnp.minimum(me, 1) + jnp.minimum(n - 1 - me, 1))

    def own(d, c):
        return part_ref.at[c, :, pl.ds(d * half, half)]

    def sum_copy(d, c, src):
        return pltpu.make_async_remote_copy(
            src_ref=src,
            dst_ref=sums.at[d, c],
            send_sem=send_sem.at[d, c],
            recv_sem=recv_sem.at[d, c],
            device_id={"wid": me + 1 if d == 0 else me - 1},
            device_id_type=pl.DeviceIdType.MESH,
        )

    def hidden_copy(d, c):
        rows = hid_ref.at[c, pl.ds(d * half, half)]
        return pltpu.make_async_remote_copy(
            src_ref=rows,
            dst_ref=rows,
            send_sem=back_sem.at[d, c],
            recv_sem=home_sem.at[d, c],
            device_id={"wid": me - 1 if d == 0 else me + 1},
            device_id_type=pl.DeviceIdType.MESH,
        )

    def summed(d, c, m):
        mine = part_ref[c, m, d * half : (d + 1) * half].astype(jnp.float32)
        return sums[d, c, m].astype(jnp.float32) + mine

    def reduce_chunk(d, c):
        place = me if d == 0 else n - 1 - me

        @pl.when(place == 0)
        def _():
            sum_copy(d, c, own(d, c)).start()

        @pl.when((place > 0) & (place < n - 1))
        def _():
            sum_copy(d, c, sums.at[d, c]).wait_recv()
            for m in range(2):
                sums[d, c, m] = summed(d, c, m).astype(sums.dtype)
            sum_copy(d, c, sums.at[d, c]).start()

        @pl.when(place == n - 1)
        def _():
            sum_copy(d, c, sums.at[d, c]).wait_recv()
            gate, up = summed(d, c, 0), summed(d, c, 1)
            hid_ref[c, d * half : (d + 1) * half] = (jax.nn.silu(gate) * up).astype(hid_ref.dtype)
            hidden_copy(d, c).start()

    def spread_chunk(d, c):
        place = me if d == 0 else n - 1 - me

        @pl.when((place > 0) & (place < n - 1))
        def _():
            hidden_copy(d, c).wait_recv()
            hidden_copy(d, c).start()

    def finish_chunk(d, c):
        place = me if d == 0 else n - 1 - me

        @pl.when(place == 0)
        def _():
            hidden_copy(d, c).wait_recv()

        @pl.when(place < n - 1)
        def _():
            sum_copy(d, c, sums.at[d, c]).wait_send()

        @pl.when(place > 0)
        def _():
            hidden_copy(d, c).wait_send()

    @pl.loop(0, chunks)
    def _(c):
        reduce_chunk(0, c)
        reduce_chunk(1, c)

        @pl.when(c >= lag)
        def _():
            spread_chunk(0, c - lag)
            spread_chunk(1, c - lag)

    @pl.loop(chunks - lag, chunks)
    def _(c):
        spread_chunk(0, c)
        spread_chunk(1, c)

    @pl.loop(0, chunks)
    def _(c):
        finish_chunk(0, c)
        finish_chunk(1, c)


def hidden_of(partial):
    n = lax.axis_size("wid")
    chunks, _, tokens, width = partial.shape
    return pl.pallas_call(
        functools.partial(hidden_kernel, n),
        out_shape=jax.ShapeDtypeStruct((chunks, tokens, width), jnp.bfloat16),
        in_specs=[pl.BlockSpec(memory_space=pltpu.VMEM)],
        out_specs=pl.BlockSpec(memory_space=pltpu.VMEM),
        scratch_shapes=[pltpu.VMEM((2, chunks, 2, tokens // 2, width), jnp.bfloat16)]
        + [pltpu.SemaphoreType.DMA((2, chunks))] * 4,
        compiler_params=pltpu.CompilerParams(
            collective_id=0, has_side_effects=True, vmem_limit_bytes=32 * 1024 * 1024
        ),
    )(partial)


def output_kernel(n, part_ref, out_ref, paired, arrived, send_1, recv_1, send_2, recv_2):
    me = lax.axis_index("ffn")
    core = lax.rem(me, 2)
    chip = me // 2
    chips = n // 2
    sibling = me + 1 - 2 * core
    others = [lax.rem(chip + 1 + i, chips) for i in range(chips - 1)]

    barrier = pltpu.get_barrier_semaphore()
    for device in [sibling] + [2 * k + core for k in others]:
        pl.semaphore_signal(
            barrier, inc=1, device_id={"ffn": device}, device_id_type=pl.DeviceIdType.MESH
        )
    pl.semaphore_wait(barrier, chips)

    first = []
    for i, k in enumerate(others + [chip]):
        copy = pltpu.make_async_remote_copy(
            src_ref=part_ref.at[2 * k + 1 - core],
            dst_ref=paired.at[i],
            send_sem=send_1.at[i],
            recv_sem=recv_1.at[i],
            device_id={"ffn": sibling},
            device_id_type=pl.DeviceIdType.MESH,
        )
        copy.start()
        first.append(copy)
    second = []
    for i, k in enumerate(others):
        first[i].wait_recv()
        mine = part_ref[2 * k + core].astype(jnp.float32)
        paired[i] = (paired[i].astype(jnp.float32) + mine).astype(paired.dtype)
        copy = pltpu.make_async_remote_copy(
            src_ref=paired.at[i],
            dst_ref=arrived.at[i],
            send_sem=send_2.at[i],
            recv_sem=recv_2.at[i],
            device_id={"ffn": 2 * k + core},
            device_id_type=pl.DeviceIdType.MESH,
        )
        copy.start()
        second.append(copy)
    first[-1].wait_recv()
    total = part_ref[me].astype(jnp.float32) + paired[chips - 1].astype(jnp.float32)
    for i, copy in enumerate(second):
        copy.wait_recv()
        total = total + arrived[i].astype(jnp.float32)
    out_ref[...] = total.astype(out_ref.dtype)
    for copy in first + second:
        copy.wait_send()


def output_of(partial):
    n = lax.axis_size("ffn")
    tokens, width = partial.shape
    chips = n // 2
    share = (tokens // n, width)
    return pl.pallas_call(
        functools.partial(output_kernel, n),
        out_shape=jax.ShapeDtypeStruct(share, jnp.bfloat16),
        in_specs=[pl.BlockSpec(memory_space=pltpu.VMEM)],
        out_specs=pl.BlockSpec(memory_space=pltpu.VMEM),
        scratch_shapes=[
            pltpu.VMEM((chips,) + share, jnp.bfloat16),
            pltpu.VMEM((chips,) + share, jnp.bfloat16),
        ]
        + [pltpu.SemaphoreType.DMA((chips,))] * 4,
        compiler_params=pltpu.CompilerParams(
            collective_id=1, has_side_effects=True, vmem_limit_bytes=32 * 1024 * 1024
        ),
    )(partial.reshape((n,) + share))


def on_device(
    tokens,
    gate_blocks,
    gate_slots,
    gate_count,
    up_blocks,
    up_slots,
    up_count,
    down_blocks,
    down_slots,
    down_count,
):
    ffn_blocks = FF // lax.axis_size("ffn") // 128
    wid_blocks = tokens.shape[1] // 128
    chunks = max(c for c in range(1, 17) if ffn_blocks % c == 0)
    full_tokens = lax.all_gather(tokens, "ffn", axis=0, tiled=True)
    partial = tile_products(
        full_tokens[None],
        [
            (gate_blocks[0, 0], gate_slots[0, 0], gate_count[0, 0]),
            (up_blocks[0, 0], up_slots[0, 0], up_count[0, 0]),
        ],
        ffn_blocks,
        chunks,
    )
    hidden = hidden_of(partial)
    mixed = tile_products(
        hidden, [(down_blocks[0, 0], down_slots[0, 0], down_count[0, 0])], wid_blocks, 1
    )
    return output_of(mixed[0, 0])


def solution(mesh):
    return jax.shard_map(
        on_device,
        mesh=mesh,
        in_specs=(
            P(("groups", "ffn"), "wid"),
            P("wid", "ffn", None, None, None),
            P("wid", "ffn", None),
            P("wid", "ffn"),
            P("wid", "ffn", None, None, None),
            P("wid", "ffn", None),
            P("wid", "ffn"),
            P("ffn", "wid", None, None, None),
            P("ffn", "wid", None),
            P("ffn", "wid"),
        ),
        out_specs=P(("groups", "ffn"), "wid"),
        check_vma=False,
    )
```

```python
import functools

import jax
import jax.numpy as jnp
from jax import lax
from jax.experimental import pallas as pl
from jax.experimental.pallas import tpu as pltpu
from jax.sharding import PartitionSpec as P

FF = 26624
GROUP = 4
BATCH = 4
STEP = GROUP * BATCH
DEPTH = 8
SUM_LAG = 2
BACK_LAG = 2


def block_lists(slots, kept, in_blocks, out_blocks):
    count = slots.shape[0]
    index = jnp.arange(count, dtype=jnp.int32)
    is_kept = index < kept
    col = jnp.where(is_kept, slots % out_blocks, out_blocks)
    row = slots // out_blocks
    rank = jnp.sum(
        (col[None, :] == col[:, None]) & (index[None, :] < index[:, None]), axis=1, dtype=jnp.int32
    )
    columns = jnp.arange(out_blocks, dtype=jnp.int32)
    number = jnp.sum(col[None, :] == columns[:, None], axis=1, dtype=jnp.int32)
    groups = (number + GROUP - 1) // GROUP
    ends = jnp.sum(
        jnp.where(columns[None, :] <= columns[:, None], groups[None, :], 0), axis=1, dtype=jnp.int32
    )
    first = jnp.sum(
        jnp.where(columns[None, :] < col[:, None], groups[None, :], 0), axis=1, dtype=jnp.int32
    )
    place = jnp.where(is_kept, first * GROUP + rank, -1)
    most = (count + out_blocks * (GROUP - 1)) // GROUP
    most = -(-most // BATCH) * BATCH
    match = place[None, :] == jnp.arange(most * GROUP, dtype=jnp.int32)[:, None]
    packed = jnp.sum(
        jnp.where(match, (index * in_blocks + row + 1)[None, :], 0), axis=1, dtype=jnp.int32
    )
    order = jnp.where(packed > 0, (packed - 1) // in_blocks, 0)
    rows = jnp.where(packed > 0, (packed - 1) % in_blocks, in_blocks)
    cols = jnp.sum(
        ends[None, :] <= jnp.arange(most, dtype=jnp.int32)[:, None], axis=1, dtype=jnp.int32
    )
    cols = jnp.minimum(cols, out_blocks - 1)
    batches = (ends[-1:] + BATCH - 1) // BATCH
    return order, rows, cols, batches


def tile_kernel(matrices, *refs):
    lists = refs[: 4 * matrices]
    x_ref = refs[4 * matrices]
    blocks = refs[4 * matrices + 1 : 5 * matrices + 1]
    out_ref, pieces, total, held, sems = refs[5 * matrices + 1 :]
    in_blocks = pieces.shape[0] - 1
    out_blocks = total.shape[0]

    def start(m, step):
        order = lists[4 * m]
        slot = lax.rem(step, DEPTH)
        for i in range(STEP):
            pltpu.make_async_copy(
                blocks[m].at[order[step * STEP + i]], held.at[m, slot, i], sems.at[m, slot]
            ).start()

    for m in range(matrices):

        @pl.loop(0, jnp.minimum(lists[4 * m + 3][0], DEPTH))
        def _(step):
            start(m, step)

    for i in range(in_blocks):
        per = x_ref.shape[2] // 128
        pieces[i] = x_ref[i // per, :, i % per * 128 : (i % per + 1) * 128]
    pieces[in_blocks] = jnp.zeros(pieces.shape[1:], pieces.dtype)

    for m in range(matrices):
        rows, cols = lists[4 * m + 1], lists[4 * m + 2]
        batches = lists[4 * m + 3][0]

        @pl.loop(0, out_blocks)
        def _(o):
            total[o] = jnp.zeros(total.shape[1:], total.dtype)

        @pl.loop(0, batches)
        def _(step):
            slot = lax.rem(step, DEPTH)
            pltpu.make_async_copy(
                blocks[m].at[pl.ds(0, STEP)], held.at[m, slot], sems.at[m, slot]
            ).wait()
            for u in range(BATCH):
                base = step * STEP + u * GROUP
                piece = jnp.concatenate([pieces[rows[base + i]] for i in range(GROUP)], axis=1)
                weight = held[m, slot, u * GROUP : (u + 1) * GROUP].reshape(GROUP * 128, 128)
                product = jnp.dot(piece, weight, preferred_element_type=jnp.float32)
                o = cols[step * BATCH + u]
                total[o] = total[o] + product

            @pl.when(step + DEPTH < batches)
            def _():
                start(m, step + DEPTH)

        for o in range(out_blocks):
            per = out_ref.shape[3] // 128
            at = o % per * 128
            out_ref[o // per, m, :, at : at + 128] = total[o].astype(out_ref.dtype)


def tile_products(operand, parts, out_blocks, chunks):
    tokens = operand.shape[1]
    in_blocks = operand.shape[0] * operand.shape[2] // 128
    matrices = len(parts)
    lists = []
    for blocks, slots, kept in parts:
        lists += block_lists(slots, kept, in_blocks, out_blocks)
    count = parts[0][0].shape[0]
    smem = pl.BlockSpec(memory_space=pltpu.SMEM)
    vmem = pl.BlockSpec(memory_space=pltpu.VMEM)
    return pl.pallas_call(
        functools.partial(tile_kernel, matrices),
        out_shape=jax.ShapeDtypeStruct(
            (chunks, matrices, tokens, out_blocks * 128 // chunks), jnp.bfloat16
        ),
        in_specs=[smem] * (4 * matrices) + [vmem] + [pl.BlockSpec(memory_space=pl.ANY)] * matrices,
        out_specs=vmem,
        scratch_shapes=[
            pltpu.VMEM((in_blocks + 1, tokens, 128), jnp.bfloat16),
            pltpu.VMEM((out_blocks, tokens, 128), jnp.float32),
            pltpu.VMEM((matrices, DEPTH, STEP, 128, 128), jnp.bfloat16),
            pltpu.SemaphoreType.DMA((matrices, DEPTH)),
        ],
        compiler_params=pltpu.CompilerParams(vmem_limit_bytes=50 * 1024 * 1024),
        cost_estimate=pl.CostEstimate(
            flops=2 * tokens * 128 * 128 * count * matrices,
            bytes_accessed=2 * 128 * 128 * count * matrices,
            transcendentals=0,
        ),
    )(*lists, operand, *[blocks for blocks, _, _ in parts])


def hidden_kernel(n, part_ref, hid_ref, sums, send_sem, recv_sem, back_sem, home_sem):
    me = lax.axis_index("wid")
    chunks, _, tokens, _ = part_ref.shape
    half = tokens // 2

    barrier = pltpu.get_barrier_semaphore()
    for exists, other in ((me > 0, me - 1), (me < n - 1, me + 1)):

        @pl.when(exists)
        def _():
            pl.semaphore_signal(
                barrier, inc=1, device_id={"wid": other}, device_id_type=pl.DeviceIdType.MESH
            )

    pl.semaphore_wait(barrier, jnp.minimum(me, 1) + jnp.minimum(n - 1 - me, 1))

    def own(d, c):
        return part_ref.at[c, :, pl.ds(d * half, half)]

    def sum_copy(d, c, src):
        return pltpu.make_async_remote_copy(
            src_ref=src,
            dst_ref=sums.at[d, c],
            send_sem=send_sem.at[d, c],
            recv_sem=recv_sem.at[d, c],
            device_id={"wid": me + 1 if d == 0 else me - 1},
            device_id_type=pl.DeviceIdType.MESH,
        )

    def hidden_copy(d, c):
        rows = hid_ref.at[c, pl.ds(d * half, half)]
        return pltpu.make_async_remote_copy(
            src_ref=rows,
            dst_ref=rows,
            send_sem=back_sem.at[d, c],
            recv_sem=home_sem.at[d, c],
            device_id={"wid": me - 1 if d == 0 else me + 1},
            device_id_type=pl.DeviceIdType.MESH,
        )

    def summed(d, c, m):
        mine = part_ref[c, m, d * half : (d + 1) * half].astype(jnp.float32)
        return sums[d, c, m].astype(jnp.float32) + mine

    def first_chunk(d, c):
        place = me if d == 0 else n - 1 - me

        @pl.when(place == 0)
        def _():
            sum_copy(d, c, own(d, c)).start()

    def reduce_chunk(d, c):
        place = me if d == 0 else n - 1 - me

        @pl.when((place > 0) & (place < n - 1))
        def _():
            sum_copy(d, c, sums.at[d, c]).wait_recv()
            for m in range(2):
                sums[d, c, m] = summed(d, c, m).astype(sums.dtype)
            sum_copy(d, c, sums.at[d, c]).start()

        @pl.when(place == n - 1)
        def _():
            sum_copy(d, c, sums.at[d, c]).wait_recv()
            gate, up = summed(d, c, 0), summed(d, c, 1)
            hid_ref[c, d * half : (d + 1) * half] = (jax.nn.silu(gate) * up).astype(hid_ref.dtype)
            hidden_copy(d, c).start()

    def spread_chunk(d, c):
        place = me if d == 0 else n - 1 - me

        @pl.when((place > 0) & (place < n - 1))
        def _():
            hidden_copy(d, c).wait_recv()
            hidden_copy(d, c).start()

    def finish_chunk(d, c):
        place = me if d == 0 else n - 1 - me

        @pl.when(place == 0)
        def _():
            hidden_copy(d, c).wait_recv()

        @pl.when(place < n - 1)
        def _():
            sum_copy(d, c, sums.at[d, c]).wait_send()

        @pl.when(place > 0)
        def _():
            hidden_copy(d, c).wait_send()

    def at(chunk, work, d):
        @pl.when((chunk >= 0) & (chunk < chunks))
        def _():
            work(d, chunk)

    @pl.loop(0, chunks + (n - 1) * (SUM_LAG + BACK_LAG))
    def _(step):
        for d in range(2):
            place = me if d == 0 else n - 1 - me
            at(step, first_chunk, d)
            at(step - place * SUM_LAG, reduce_chunk, d)
            at(step - (n - 1) * SUM_LAG - (n - 1 - place) * BACK_LAG, spread_chunk, d)

    @pl.loop(0, chunks)
    def _(c):
        finish_chunk(0, c)
        finish_chunk(1, c)


def hidden_of(partial):
    n = lax.axis_size("wid")
    chunks, _, tokens, width = partial.shape
    return pl.pallas_call(
        functools.partial(hidden_kernel, n),
        out_shape=jax.ShapeDtypeStruct((chunks, tokens, width), jnp.bfloat16),
        in_specs=[pl.BlockSpec(memory_space=pltpu.VMEM)],
        out_specs=pl.BlockSpec(memory_space=pltpu.VMEM),
        scratch_shapes=[pltpu.VMEM((2, chunks, 2, tokens // 2, width), jnp.bfloat16)]
        + [pltpu.SemaphoreType.DMA((2, chunks))] * 4,
        compiler_params=pltpu.CompilerParams(
            collective_id=0, has_side_effects=True, vmem_limit_bytes=32 * 1024 * 1024
        ),
    )(partial)


def output_kernel(n, part_ref, out_ref, paired, arrived, send_1, recv_1, send_2, recv_2):
    me = lax.axis_index("ffn")
    core = lax.rem(me, 2)
    chip = me // 2
    chips = n // 2
    sibling = me + 1 - 2 * core
    others = [lax.rem(chip + 1 + i, chips) for i in range(chips - 1)]

    barrier = pltpu.get_barrier_semaphore()
    for device in [sibling] + [2 * k + core for k in others]:
        pl.semaphore_signal(
            barrier, inc=1, device_id={"ffn": device}, device_id_type=pl.DeviceIdType.MESH
        )
    pl.semaphore_wait(barrier, chips)

    first = []
    for i, k in enumerate(others + [chip]):
        copy = pltpu.make_async_remote_copy(
            src_ref=part_ref.at[2 * k + 1 - core],
            dst_ref=paired.at[i],
            send_sem=send_1.at[i],
            recv_sem=recv_1.at[i],
            device_id={"ffn": sibling},
            device_id_type=pl.DeviceIdType.MESH,
        )
        copy.start()
        first.append(copy)
    second = []
    for i, k in enumerate(others):
        first[i].wait_recv()
        mine = part_ref[2 * k + core].astype(jnp.float32)
        paired[i] = (paired[i].astype(jnp.float32) + mine).astype(paired.dtype)
        copy = pltpu.make_async_remote_copy(
            src_ref=paired.at[i],
            dst_ref=arrived.at[i],
            send_sem=send_2.at[i],
            recv_sem=recv_2.at[i],
            device_id={"ffn": 2 * k + core},
            device_id_type=pl.DeviceIdType.MESH,
        )
        copy.start()
        second.append(copy)
    first[-1].wait_recv()
    total = part_ref[me].astype(jnp.float32) + paired[chips - 1].astype(jnp.float32)
    for i, copy in enumerate(second):
        copy.wait_recv()
        total = total + arrived[i].astype(jnp.float32)
    out_ref[...] = total.astype(out_ref.dtype)
    for copy in first + second:
        copy.wait_send()


def output_of(partial):
    n = lax.axis_size("ffn")
    tokens, width = partial.shape
    chips = n // 2
    share = (tokens // n, width)
    return pl.pallas_call(
        functools.partial(output_kernel, n),
        out_shape=jax.ShapeDtypeStruct(share, jnp.bfloat16),
        in_specs=[pl.BlockSpec(memory_space=pltpu.VMEM)],
        out_specs=pl.BlockSpec(memory_space=pltpu.VMEM),
        scratch_shapes=[
            pltpu.VMEM((chips,) + share, jnp.bfloat16),
            pltpu.VMEM((chips,) + share, jnp.bfloat16),
        ]
        + [pltpu.SemaphoreType.DMA((chips,))] * 4,
        compiler_params=pltpu.CompilerParams(
            collective_id=1, has_side_effects=True, vmem_limit_bytes=32 * 1024 * 1024
        ),
    )(partial.reshape((n,) + share))


def on_device(
    tokens,
    gate_blocks,
    gate_slots,
    gate_count,
    up_blocks,
    up_slots,
    up_count,
    down_blocks,
    down_slots,
    down_count,
):
    ffn_blocks = FF // lax.axis_size("ffn") // 128
    wid_blocks = tokens.shape[1] // 128
    chunks = max(c for c in range(1, 17) if ffn_blocks % c == 0)
    full_tokens = lax.all_gather(tokens, "ffn", axis=0, tiled=True)
    partial = tile_products(
        full_tokens[None],
        [
            (gate_blocks[0, 0], gate_slots[0, 0], gate_count[0, 0]),
            (up_blocks[0, 0], up_slots[0, 0], up_count[0, 0]),
        ],
        ffn_blocks,
        chunks,
    )
    hidden = hidden_of(partial)
    mixed = tile_products(
        hidden, [(down_blocks[0, 0], down_slots[0, 0], down_count[0, 0])], wid_blocks, 1
    )
    return output_of(mixed[0, 0])


def solution(mesh):
    return jax.shard_map(
        on_device,
        mesh=mesh,
        in_specs=(
            P(("groups", "ffn"), "wid"),
            P("wid", "ffn", None, None, None),
            P("wid", "ffn", None),
            P("wid", "ffn"),
            P("wid", "ffn", None, None, None),
            P("wid", "ffn", None),
            P("wid", "ffn"),
            P("ffn", "wid", None, None, None),
            P("ffn", "wid", None),
            P("ffn", "wid"),
        ),
        out_specs=P(("groups", "ffn"), "wid"),
        check_vma=False,
    )
```

```python
import functools

import jax
import jax.numpy as jnp
from jax import lax
from jax.experimental import pallas as pl
from jax.experimental.pallas import tpu as pltpu
from jax.sharding import PartitionSpec as P

FF = 26624
GROUP = 4
BATCH = 8
STEP = GROUP * BATCH
DEPTH = 6
SUM_LAG = 2
BACK_LAG = 2


def block_lists(slots, kept, in_blocks, out_blocks):
    count = slots.shape[0]
    index = jnp.arange(count, dtype=jnp.int32)
    is_kept = index < kept
    col = jnp.where(is_kept, slots % out_blocks, out_blocks)
    row = slots // out_blocks
    rank = jnp.sum(
        (col[None, :] == col[:, None]) & (index[None, :] < index[:, None]), axis=1, dtype=jnp.int32
    )
    columns = jnp.arange(out_blocks, dtype=jnp.int32)
    number = jnp.sum(col[None, :] == columns[:, None], axis=1, dtype=jnp.int32)
    groups = (number + GROUP - 1) // GROUP
    ends = jnp.sum(
        jnp.where(columns[None, :] <= columns[:, None], groups[None, :], 0), axis=1, dtype=jnp.int32
    )
    first = jnp.sum(
        jnp.where(columns[None, :] < col[:, None], groups[None, :], 0), axis=1, dtype=jnp.int32
    )
    place = jnp.where(is_kept, first * GROUP + rank, -1)
    most = (count + out_blocks * (GROUP - 1)) // GROUP
    most = -(-most // BATCH) * BATCH
    match = place[None, :] == jnp.arange(most * GROUP, dtype=jnp.int32)[:, None]
    packed = jnp.sum(
        jnp.where(match, (index * in_blocks + row + 1)[None, :], 0), axis=1, dtype=jnp.int32
    )
    order = jnp.where(packed > 0, (packed - 1) // in_blocks, 0)
    rows = jnp.where(packed > 0, (packed - 1) % in_blocks, in_blocks)
    cols = jnp.sum(
        ends[None, :] <= jnp.arange(most, dtype=jnp.int32)[:, None], axis=1, dtype=jnp.int32
    )
    cols = jnp.minimum(cols, out_blocks - 1)
    batches = (ends[-1:] + BATCH - 1) // BATCH
    return order, rows, cols, batches


def tile_kernel(matrices, *refs):
    lists = refs[: 4 * matrices]
    x_ref = refs[4 * matrices]
    blocks = refs[4 * matrices + 1 : 5 * matrices + 1]
    out_ref, pieces, total, held, sems = refs[5 * matrices + 1 :]
    in_blocks = pieces.shape[0] - 1
    out_blocks = total.shape[0]

    def start(m, step):
        order = lists[4 * m]
        slot = lax.rem(step, DEPTH)
        for i in range(STEP):
            pltpu.make_async_copy(
                blocks[m].at[order[step * STEP + i]], held.at[m, slot, i], sems.at[m, slot]
            ).start()

    for m in range(matrices):

        @pl.loop(0, jnp.minimum(lists[4 * m + 3][0], DEPTH))
        def _(step):
            start(m, step)

    for i in range(in_blocks):
        per = x_ref.shape[2] // 128
        pieces[i] = x_ref[i // per, :, i % per * 128 : (i % per + 1) * 128]
    pieces[in_blocks] = jnp.zeros(pieces.shape[1:], pieces.dtype)

    for m in range(matrices):
        rows, cols = lists[4 * m + 1], lists[4 * m + 2]
        batches = lists[4 * m + 3][0]

        @pl.loop(0, out_blocks)
        def _(o):
            total[o] = jnp.zeros(total.shape[1:], total.dtype)

        @pl.loop(0, batches)
        def _(step):
            slot = lax.rem(step, DEPTH)
            pltpu.make_async_copy(
                blocks[m].at[pl.ds(0, STEP)], held.at[m, slot], sems.at[m, slot]
            ).wait()
            for u in range(BATCH):
                base = step * STEP + u * GROUP
                piece = jnp.concatenate([pieces[rows[base + i]] for i in range(GROUP)], axis=1)
                weight = held[m, slot, u * GROUP : (u + 1) * GROUP].reshape(GROUP * 128, 128)
                product = jnp.dot(piece, weight, preferred_element_type=jnp.float32)
                o = cols[step * BATCH + u]
                total[o] = total[o] + product

            @pl.when(step + DEPTH < batches)
            def _():
                start(m, step + DEPTH)

        for o in range(out_blocks):
            per = out_ref.shape[3] // 128
            at = o % per * 128
            out_ref[o // per, m, :, at : at + 128] = total[o].astype(out_ref.dtype)


def tile_products(operand, parts, out_blocks, chunks):
    tokens = operand.shape[1]
    in_blocks = operand.shape[0] * operand.shape[2] // 128
    matrices = len(parts)
    lists = []
    for blocks, slots, kept in parts:
        lists += block_lists(slots, kept, in_blocks, out_blocks)
    count = parts[0][0].shape[0]
    smem = pl.BlockSpec(memory_space=pltpu.SMEM)
    vmem = pl.BlockSpec(memory_space=pltpu.VMEM)
    return pl.pallas_call(
        functools.partial(tile_kernel, matrices),
        out_shape=jax.ShapeDtypeStruct(
            (chunks, matrices, tokens, out_blocks * 128 // chunks), jnp.bfloat16
        ),
        in_specs=[smem] * (4 * matrices) + [vmem] + [pl.BlockSpec(memory_space=pl.ANY)] * matrices,
        out_specs=vmem,
        scratch_shapes=[
            pltpu.VMEM((in_blocks + 1, tokens, 128), jnp.bfloat16),
            pltpu.VMEM((out_blocks, tokens, 128), jnp.float32),
            pltpu.VMEM((matrices, DEPTH, STEP, 128, 128), jnp.bfloat16),
            pltpu.SemaphoreType.DMA((matrices, DEPTH)),
        ],
        compiler_params=pltpu.CompilerParams(vmem_limit_bytes=50 * 1024 * 1024),
        cost_estimate=pl.CostEstimate(
            flops=2 * tokens * 128 * 128 * count * matrices,
            bytes_accessed=2 * 128 * 128 * count * matrices,
            transcendentals=0,
        ),
    )(*lists, operand, *[blocks for blocks, _, _ in parts])


def hidden_kernel(n, part_ref, hid_ref, sums, send_sem, recv_sem, back_sem, home_sem):
    me = lax.axis_index("wid")
    chunks, _, tokens, _ = part_ref.shape
    half = tokens // 2

    barrier = pltpu.get_barrier_semaphore()
    for exists, other in ((me > 0, me - 1), (me < n - 1, me + 1)):

        @pl.when(exists)
        def _():
            pl.semaphore_signal(
                barrier, inc=1, device_id={"wid": other}, device_id_type=pl.DeviceIdType.MESH
            )

    pl.semaphore_wait(barrier, jnp.minimum(me, 1) + jnp.minimum(n - 1 - me, 1))

    def own(d, c):
        return part_ref.at[c, :, pl.ds(d * half, half)]

    def sum_copy(d, c, src):
        return pltpu.make_async_remote_copy(
            src_ref=src,
            dst_ref=sums.at[d, c],
            send_sem=send_sem.at[d, c],
            recv_sem=recv_sem.at[d, c],
            device_id={"wid": me + 1 if d == 0 else me - 1},
            device_id_type=pl.DeviceIdType.MESH,
        )

    def hidden_copy(d, c):
        rows = hid_ref.at[c, pl.ds(d * half, half)]
        return pltpu.make_async_remote_copy(
            src_ref=rows,
            dst_ref=rows,
            send_sem=back_sem.at[d, c],
            recv_sem=home_sem.at[d, c],
            device_id={"wid": me - 1 if d == 0 else me + 1},
            device_id_type=pl.DeviceIdType.MESH,
        )

    def summed(d, c, m):
        mine = part_ref[c, m, d * half : (d + 1) * half].astype(jnp.float32)
        return sums[d, c, m].astype(jnp.float32) + mine

    def first_chunk(d, c):
        place = me if d == 0 else n - 1 - me

        @pl.when(place == 0)
        def _():
            sum_copy(d, c, own(d, c)).start()

    def reduce_chunk(d, c):
        place = me if d == 0 else n - 1 - me

        @pl.when((place > 0) & (place < n - 1))
        def _():
            sum_copy(d, c, sums.at[d, c]).wait_recv()
            for m in range(2):
                sums[d, c, m] = summed(d, c, m).astype(sums.dtype)
            sum_copy(d, c, sums.at[d, c]).start()

        @pl.when(place == n - 1)
        def _():
            sum_copy(d, c, sums.at[d, c]).wait_recv()
            gate, up = summed(d, c, 0), summed(d, c, 1)
            hid_ref[c, d * half : (d + 1) * half] = (jax.nn.silu(gate) * up).astype(hid_ref.dtype)
            hidden_copy(d, c).start()

    def spread_chunk(d, c):
        place = me if d == 0 else n - 1 - me

        @pl.when((place > 0) & (place < n - 1))
        def _():
            hidden_copy(d, c).wait_recv()
            hidden_copy(d, c).start()

    def finish_chunk(d, c):
        place = me if d == 0 else n - 1 - me

        @pl.when(place == 0)
        def _():
            hidden_copy(d, c).wait_recv()

        @pl.when(place < n - 1)
        def _():
            sum_copy(d, c, sums.at[d, c]).wait_send()

        @pl.when(place > 0)
        def _():
            hidden_copy(d, c).wait_send()

    def at(chunk, work, d):
        @pl.when((chunk >= 0) & (chunk < chunks))
        def _():
            work(d, chunk)

    @pl.loop(0, chunks + (n - 1) * (SUM_LAG + BACK_LAG))
    def _(step):
        for d in range(2):
            place = me if d == 0 else n - 1 - me
            at(step, first_chunk, d)
            at(step - place * SUM_LAG, reduce_chunk, d)
            at(step - (n - 1) * SUM_LAG - (n - 1 - place) * BACK_LAG, spread_chunk, d)

    @pl.loop(0, chunks)
    def _(c):
        finish_chunk(0, c)
        finish_chunk(1, c)


def hidden_of(partial):
    n = lax.axis_size("wid")
    chunks, _, tokens, width = partial.shape
    return pl.pallas_call(
        functools.partial(hidden_kernel, n),
        out_shape=jax.ShapeDtypeStruct((chunks, tokens, width), jnp.bfloat16),
        in_specs=[pl.BlockSpec(memory_space=pltpu.VMEM)],
        out_specs=pl.BlockSpec(memory_space=pltpu.VMEM),
        scratch_shapes=[pltpu.VMEM((2, chunks, 2, tokens // 2, width), jnp.bfloat16)]
        + [pltpu.SemaphoreType.DMA((2, chunks))] * 4,
        compiler_params=pltpu.CompilerParams(
            collective_id=0, has_side_effects=True, vmem_limit_bytes=32 * 1024 * 1024
        ),
    )(partial)


def output_kernel(n, part_ref, out_ref, paired, arrived, send_1, recv_1, send_2, recv_2):
    me = lax.axis_index("ffn")
    core = lax.rem(me, 2)
    chip = me // 2
    chips = n // 2
    sibling = me + 1 - 2 * core
    others = [lax.rem(chip + 1 + i, chips) for i in range(chips - 1)]

    barrier = pltpu.get_barrier_semaphore()
    for device in [sibling] + [2 * k + core for k in others]:
        pl.semaphore_signal(
            barrier, inc=1, device_id={"ffn": device}, device_id_type=pl.DeviceIdType.MESH
        )
    pl.semaphore_wait(barrier, chips)

    first = []
    for i, k in enumerate(others + [chip]):
        copy = pltpu.make_async_remote_copy(
            src_ref=part_ref.at[2 * k + 1 - core],
            dst_ref=paired.at[i],
            send_sem=send_1.at[i],
            recv_sem=recv_1.at[i],
            device_id={"ffn": sibling},
            device_id_type=pl.DeviceIdType.MESH,
        )
        copy.start()
        first.append(copy)
    second = []
    for i, k in enumerate(others):
        first[i].wait_recv()
        mine = part_ref[2 * k + core].astype(jnp.float32)
        paired[i] = (paired[i].astype(jnp.float32) + mine).astype(paired.dtype)
        copy = pltpu.make_async_remote_copy(
            src_ref=paired.at[i],
            dst_ref=arrived.at[i],
            send_sem=send_2.at[i],
            recv_sem=recv_2.at[i],
            device_id={"ffn": 2 * k + core},
            device_id_type=pl.DeviceIdType.MESH,
        )
        copy.start()
        second.append(copy)
    first[-1].wait_recv()
    total = part_ref[me].astype(jnp.float32) + paired[chips - 1].astype(jnp.float32)
    for i, copy in enumerate(second):
        copy.wait_recv()
        total = total + arrived[i].astype(jnp.float32)
    out_ref[...] = total.astype(out_ref.dtype)
    for copy in first + second:
        copy.wait_send()


def output_of(partial):
    n = lax.axis_size("ffn")
    tokens, width = partial.shape
    chips = n // 2
    share = (tokens // n, width)
    return pl.pallas_call(
        functools.partial(output_kernel, n),
        out_shape=jax.ShapeDtypeStruct(share, jnp.bfloat16),
        in_specs=[pl.BlockSpec(memory_space=pltpu.VMEM)],
        out_specs=pl.BlockSpec(memory_space=pltpu.VMEM),
        scratch_shapes=[
            pltpu.VMEM((chips,) + share, jnp.bfloat16),
            pltpu.VMEM((chips,) + share, jnp.bfloat16),
        ]
        + [pltpu.SemaphoreType.DMA((chips,))] * 4,
        compiler_params=pltpu.CompilerParams(
            collective_id=1, has_side_effects=True, vmem_limit_bytes=32 * 1024 * 1024
        ),
    )(partial.reshape((n,) + share))


def on_device(
    tokens,
    gate_blocks,
    gate_slots,
    gate_count,
    up_blocks,
    up_slots,
    up_count,
    down_blocks,
    down_slots,
    down_count,
):
    ffn_blocks = FF // lax.axis_size("ffn") // 128
    wid_blocks = tokens.shape[1] // 128
    chunks = max(c for c in range(1, 17) if ffn_blocks % c == 0)
    full_tokens = lax.all_gather(tokens, "ffn", axis=0, tiled=True)
    partial = tile_products(
        full_tokens[None],
        [
            (gate_blocks[0, 0], gate_slots[0, 0], gate_count[0, 0]),
            (up_blocks[0, 0], up_slots[0, 0], up_count[0, 0]),
        ],
        ffn_blocks,
        chunks,
    )
    hidden = hidden_of(partial)
    mixed = tile_products(
        hidden, [(down_blocks[0, 0], down_slots[0, 0], down_count[0, 0])], wid_blocks, 1
    )
    return output_of(mixed[0, 0])


def solution(mesh):
    return jax.shard_map(
        on_device,
        mesh=mesh,
        in_specs=(
            P(("groups", "ffn"), "wid"),
            P("wid", "ffn", None, None, None),
            P("wid", "ffn", None),
            P("wid", "ffn"),
            P("wid", "ffn", None, None, None),
            P("wid", "ffn", None),
            P("wid", "ffn"),
            P("ffn", "wid", None, None, None),
            P("ffn", "wid", None),
            P("ffn", "wid"),
        ),
        out_specs=P(("groups", "ffn"), "wid"),
        check_vma=False,
    )
```
